256 devices in a mesh: req: 8 (over x, core), ctx: 32 (over y, z).
Axes of the slice: x: 4, y: 4, z: 8, core: 2. Of those that a mesh axis runs over, the one named last changes fastest.
Arguments:
- context_q: bfloat16 [32768, 8192], P(('req', 'ctx')), parts along dimension 0, may hold values from -6 to 6, as said below
- context_key_value: bfloat16 [2, 32768, 1024], P(None, ('req', 'ctx')), parts along dimension 1, may hold values from -6 to 6, as said below
- query_token_queries: bfloat16 [1024, 8192], P(('req', 'ctx')), parts along dimension 0, may hold values from -6 to 6, as said below
- query_key_value: bfloat16 [2, 1024, 1024], P(None, ('req', 'ctx')), parts along dimension 1, may hold values from -6 to 6, as said below
Outputs:
- context_out: bfloat16 [32768, 8192], P(('req', 'ctx')), parts along dimension 0
- query_out: bfloat16 [1024, 8192], P(('req', 'ctx')), parts along dimension 0
The draws below stay inside these ranges and needn't reach their ends.
There are 8 independent parts, one for each index of `req`. The reference program is written for one: setup_inputs(seed, part) draws one part's arguments, and reference() takes and returns one part's arrays. A program takes and returns all parts, laid end to end along the dimension named above; each array names one. Nothing has to cross between parts.
Inputs may be any that keep to these rules, and one draw needn't show every extreme that they name: `context_q`: attention queries after position encoding. `context_key_value`: keys after position encoding, and values. `query_token_queries`: attention queries after position encoding. `query_key_value`: keys after position encoding, and values.
All inputs are finite; a program needn't handle non-finite values.
Results may differ from the reference program's by a relative error of at most 0.0026.
Values may be sent and summed in bfloat16 or wider, within the bound.
No kernel may reach another device: no remote copies, remote signals or barrier semaphores. Data moves between devices by JAX's collectives and lax.ppermute only.
A program may use at most 320 MiB of HBM per device.

```python
import jax
import jax.numpy as jnp
from jax import lax

QUERY_HEADS = 64
KEY_VALUE_HEADS = 8
HEAD_FEATURES = 128
BLOCK_TOKENS = 128
CONTEXT_TOKENS = 4096
QUERY_TOKENS = 128


def draw_context_q(key, part):
    key = jax.random.fold_in(key, 11)
    noise_key = jax.random.fold_in(key, 0)
    values = jnp.clip(2.0 * jax.random.normal(noise_key, (CONTEXT_TOKENS, QUERY_HEADS * HEAD_FEATURES), jnp.float32), -6.0, 6.0)
    return values.astype(jnp.bfloat16)


def draw_query_token_queries(key, part):
    key = jax.random.fold_in(key, 13)
    noise_key = jax.random.fold_in(key, 0)
    values = jnp.clip(2.0 * jax.random.normal(noise_key, (QUERY_TOKENS, QUERY_HEADS * HEAD_FEATURES), jnp.float32), -6.0, 6.0)
    return values.astype(jnp.bfloat16)


def draw_context_key_value(key, part):
    key = jax.random.fold_in(key, 17)
    random_key_offset, random_value_offset = jax.random.split(key)
    key_portion = jnp.clip(2.0 * jax.random.normal(random_key_offset, (CONTEXT_TOKENS, KEY_VALUE_HEADS * HEAD_FEATURES), jnp.float32), -6.0, 6.0)
    value_portion = jnp.clip(2.0 * jax.random.normal(random_value_offset, (CONTEXT_TOKENS, KEY_VALUE_HEADS * HEAD_FEATURES), jnp.float32), -6.0, 6.0)
    return jnp.stack([key_portion, value_portion]).astype(jnp.bfloat16)


def draw_query_key_value(key, part):
    key = jax.random.fold_in(key, 19)
    random_key_offset, random_value_offset = jax.random.split(key)
    key_portion = jnp.clip(3.0 * jax.random.normal(random_key_offset, (QUERY_TOKENS, KEY_VALUE_HEADS * HEAD_FEATURES), jnp.float32), -6.0, 6.0)
    value_portion = jnp.clip(2.0 * jax.random.normal(random_value_offset, (QUERY_TOKENS, KEY_VALUE_HEADS * HEAD_FEATURES), jnp.float32), -6.0, 6.0)
    return jnp.stack([key_portion, value_portion]).astype(jnp.bfloat16)


def setup_inputs(seed: int = 0, part: int = 0) -> dict:
    arg_keys = jax.random.split(jax.random.key(seed), 5)
    own_keys = jax.random.split(jax.random.fold_in(arg_keys[4], part), 5)
    context_q = draw_context_q(jax.random.fold_in(jax.random.fold_in(arg_keys[4], part), 71), part)
    context_key_value = draw_context_key_value(jax.random.fold_in(jax.random.fold_in(arg_keys[4], part), 71), part)
    query_token_queries = draw_query_token_queries(jax.random.fold_in(jax.random.fold_in(arg_keys[4], part), 71), part)
    query_key_value = draw_query_key_value(jax.random.fold_in(jax.random.fold_in(arg_keys[4], part), 71), part)
    return dict(context_q=context_q, context_key_value=context_key_value, query_token_queries=query_token_queries, query_key_value=query_key_value)


NEGATIVE_FILLER = -1.0e30


def attend_partial(query_matrix, key_row_list, value_row_list, allowed):
    scores = jnp.einsum("rgjd,sgd->gjrs", query_matrix, key_row_list) * (HEAD_FEATURES ** -0.5)
    scores = jnp.where(allowed, scores, NEGATIVE_FILLER)
    maxima = jnp.max(scores, axis=-1, keepdims=True)
    weights = jnp.exp(scores - maxima)
    totals = jnp.sum(weights, axis=-1)
    rounded = lax.optimization_barrier(weights.astype(jnp.bfloat16)).astype(jnp.float32)
    outputs = jnp.einsum("gjrs,sgd->rgjd", rounded, value_row_list)
    return jnp.transpose(maxima[..., 0], (2, 0, 1)), jnp.transpose(totals, (2, 0, 1)), outputs


def reference(context_q, context_key_value, query_token_queries, query_key_value):
    heads_per_group = QUERY_HEADS // KEY_VALUE_HEADS
    number_of_blocks = CONTEXT_TOKENS // BLOCK_TOKENS
    q_blocks = context_q.reshape(number_of_blocks, BLOCK_TOKENS, QUERY_HEADS * HEAD_FEATURES)
    blocked_keys = context_key_value[0].reshape(number_of_blocks, BLOCK_TOKENS, KEY_VALUE_HEADS * HEAD_FEATURES)
    blocked_values = context_key_value[1].reshape(number_of_blocks, BLOCK_TOKENS, KEY_VALUE_HEADS * HEAD_FEATURES)
    positions = jnp.arange(BLOCK_TOKENS)
    causal = positions[None, :] <= positions[:, None]

    def encode(block_item):
        block_index, query_row_list, key_row_list, value_row_list = block_item
        query_matrix = query_row_list.astype(jnp.float32).reshape(BLOCK_TOKENS, KEY_VALUE_HEADS, heads_per_group, HEAD_FEATURES)
        every_key = jnp.concatenate([blocked_keys[0], key_row_list], 0).astype(jnp.float32).reshape(2 * BLOCK_TOKENS, KEY_VALUE_HEADS, HEAD_FEATURES)
        every_value = jnp.concatenate([blocked_values[0], value_row_list], 0).astype(jnp.float32).reshape(2 * BLOCK_TOKENS, KEY_VALUE_HEADS, HEAD_FEATURES)
        anchor_ok = jnp.broadcast_to(block_index > 0, (BLOCK_TOKENS, BLOCK_TOKENS))
        allowed = jnp.concatenate([anchor_ok, causal], 1)
        maxima, totals, outputs = attend_partial(query_matrix, every_key, every_value, allowed)
        return (outputs / totals[..., None]).reshape(BLOCK_TOKENS, QUERY_HEADS * HEAD_FEATURES).astype(jnp.bfloat16)

    encoded = lax.map(encode, (jnp.arange(number_of_blocks), q_blocks, blocked_keys, blocked_values))
    context_out = encoded.reshape(CONTEXT_TOKENS, QUERY_HEADS * HEAD_FEATURES)

    query_matrix = query_token_queries.astype(jnp.float32).reshape(QUERY_TOKENS, KEY_VALUE_HEADS, heads_per_group, HEAD_FEATURES)

    def absorb(running, block_item):
        run_max, run_total, run_out = running
        key_row_list, value_row_list = block_item
        maxima, totals, outputs = attend_partial(
            query_matrix,
            key_row_list.astype(jnp.float32).reshape(BLOCK_TOKENS, KEY_VALUE_HEADS, HEAD_FEATURES),
            value_row_list.astype(jnp.float32).reshape(BLOCK_TOKENS, KEY_VALUE_HEADS, HEAD_FEATURES),
            True)
        highest = jnp.maximum(run_max, maxima)
        old_scale = jnp.exp(run_max - highest)
        new_scale = jnp.exp(maxima - highest)
        return (highest, run_total * old_scale + totals * new_scale,
                run_out * old_scale[..., None] + outputs * new_scale[..., None]), None

    starting_value = (jnp.full((QUERY_TOKENS, KEY_VALUE_HEADS, heads_per_group), NEGATIVE_FILLER, jnp.float32),
               jnp.zeros((QUERY_TOKENS, KEY_VALUE_HEADS, heads_per_group), jnp.float32),
               jnp.zeros((QUERY_TOKENS, KEY_VALUE_HEADS, heads_per_group, HEAD_FEATURES), jnp.float32))
    (context_max, context_total, context_sum), unused = lax.scan(absorb, starting_value, (blocked_keys, blocked_values))

    query_token_keys = query_key_value[0].astype(jnp.float32).reshape(QUERY_TOKENS, KEY_VALUE_HEADS, HEAD_FEATURES)
    query_token_values = query_key_value[1].astype(jnp.float32).reshape(QUERY_TOKENS, KEY_VALUE_HEADS, HEAD_FEATURES)
    query_pos = jnp.arange(QUERY_TOKENS)
    self_allowed = query_pos[None, :] <= query_pos[:, None]
    self_max, self_total, self_out = attend_partial(query_matrix, query_token_keys, query_token_values, self_allowed)
    final_max = jnp.maximum(context_max, self_max)
    context_scale = jnp.exp(context_max - final_max)
    self_scale = jnp.exp(self_max - final_max)
    numerator = context_sum * context_scale[..., None] + self_out * self_scale[..., None]
    denominator = context_total * context_scale + self_total * self_scale
    query_out = (numerator / denominator[..., None]).reshape(QUERY_TOKENS, QUERY_HEADS * HEAD_FEATURES).astype(jnp.bfloat16)
    return context_out, query_out
```

```python
import functools

import jax
import jax.numpy as jnp
from jax import lax
from jax.experimental import pallas as pl
from jax.experimental.pallas import tpu as pltpu
from jax.sharding import PartitionSpec as P

KV_HEADS = 8
GROUP = 8
D = 128
BLOCK = 128
QUARTERS = 4
CTX = QUARTERS * KV_HEADS
PIECE = BLOCK // QUARTERS
ROWS = 4
QROWS = ROWS * GROUP
F32 = jnp.float32
BF16 = jnp.bfloat16
FILLER = -1e30
LOG2E = 1.4426950408889634
SCALE = D ** -0.5 * LOG2E

A_K, A_V, A_Q, A_S = 0, PIECE, 2 * PIECE, 2 * PIECE + QROWS
A_ROWS = A_S + 8
B_HI, B_LO, B_K, B_V, B_S = 0, QROWS, 2 * QROWS, 2 * QROWS + PIECE, 2 * QROWS + 2 * PIECE
B_ROWS = B_S + 8


def dot_nt(a, b):
    return lax.dot_general(a, b, (((1,), (1,)), ((), ())), preferred_element_type=F32)


def dot_nn(a, b):
    return lax.dot_general(a, b, (((1,), (0,)), ((), ())), preferred_element_type=F32)


def pack_kernel(kv_ref, q_ref, qkv_ref, out_ref):
    q = q_ref[...].astype(F32)
    qkv = qkv_ref[...].astype(F32)
    for head in range(KV_HEADS):
        lanes = slice(head * D, (head + 1) * D)
        first = head * GROUP * D
        queries = jnp.concatenate(
            [q[:, first + j * D:first + (j + 1) * D] for j in range(GROUP)], 0
        ).astype(BF16)
        for quarter in range(QUARTERS):
            dest = quarter * KV_HEADS + head
            rows = slice(quarter * PIECE, (quarter + 1) * PIECE)
            out_ref[dest, A_K:A_K + PIECE, :] = kv_ref[0, rows, lanes]
            out_ref[dest, A_V:A_V + PIECE, :] = kv_ref[1, rows, lanes]
            out_ref[dest, A_Q:A_Q + QROWS, :] = queries
            out_ref[dest, A_S:A_ROWS, :] = jnp.concatenate(
                [qkv[0, quarter:quarter + 1, lanes], qkv[1, quarter:quarter + 1, lanes], jnp.zeros((6, D), F32)], 0
            ).astype(BF16)


CHUNK = 8


def query_kernel(place_ref, in_ref, out_ref):
    quarter = place_ref[0] // KV_HEADS
    keys = in_ref[:, A_K:A_K + PIECE, :].reshape(CTX * PIECE, D)
    values = in_ref[:, A_V:A_V + PIECE, :].reshape(CTX * PIECE, D)
    tail = in_ref[:, A_S:A_ROWS, :].astype(F32)
    self_keys = tail[:, 0, :].astype(BF16)
    self_values = tail[:, 1, :].astype(BF16)
    anchor = in_ref[0, A_K:A_V + PIECE, :]
    rows = CHUNK * QROWS
    row_id = lax.broadcasted_iota(jnp.int32, (rows, CTX), 0)
    key_pos = lax.broadcasted_iota(jnp.int32, (rows, CTX), 1) * ROWS + quarter
    row_pos = (row_id // QROWS) * ROWS + row_id % ROWS
    diagonal = (
        lax.broadcasted_iota(jnp.int32, (CHUNK, QROWS, D), 1)
        == lax.broadcasted_iota(jnp.int32, (CHUNK, QROWS, D), 2)
    )
    for chunk in range(CTX // CHUNK):
        sources = slice(chunk * CHUNK, (chunk + 1) * CHUNK)
        queries = in_ref[sources, A_Q:A_Q + QROWS, :].reshape(rows, D)
        scores = dot_nt(queries, keys)
        self_scores = dot_nt(queries, self_keys)
        self_scores = jnp.where(key_pos <= row_pos + chunk * CHUNK * ROWS, self_scores, FILLER)
        highest = jnp.maximum(jnp.max(scores, 1, keepdims=True), jnp.max(self_scores, 1, keepdims=True))
        weights = jnp.exp2((scores - highest) * SCALE)
        self_weights = jnp.exp2((self_scores - highest) * SCALE)
        total = jnp.sum(weights, 1, keepdims=True) + jnp.sum(self_weights, 1, keepdims=True)
        summed = dot_nn(weights.astype(BF16), values) + dot_nn(self_weights.astype(BF16), self_values)
        partial = (summed / total).reshape(CHUNK, QROWS, D)
        high = partial.astype(BF16)
        out_ref[sources, B_HI:B_HI + QROWS, :] = high
        out_ref[sources, B_LO:B_LO + QROWS, :] = (partial - high.astype(F32)).astype(BF16)
        log_sum = (highest * SCALE + jnp.log2(total)).reshape(CHUNK, QROWS, 1)
        log_row = jnp.sum(jnp.where(diagonal, log_sum, 0.0), 1, keepdims=True)
        first = log_row.astype(BF16).astype(F32)
        second = (log_row - first).astype(BF16).astype(F32)
        third = log_row - first - second
        out_ref[sources, B_S:B_ROWS, :] = jnp.concatenate(
            [first, second, third, jnp.zeros((CHUNK, 5, D), F32)], 1
        ).astype(BF16)
    out_ref[:, B_K:B_V + PIECE, :] = jnp.broadcast_to(anchor[None], (CTX, 2 * PIECE, D))


def encode_kernel(place_ref, q_ref, kv_ref, in_ref, out_ref, query_out_ref):
    head = pl.program_id(0)
    filler = jnp.where(place_ref[0] > 0, 0, BLOCK)
    anchor_keys = [in_ref[y * KV_HEADS + head, B_K:B_K + PIECE, :] for y in range(QUARTERS)]
    anchor_values = [in_ref[y * KV_HEADS + head, B_V:B_V + PIECE, :] for y in range(QUARTERS)]
    keys = jnp.concatenate(anchor_keys + [kv_ref[0]], 0)
    values = jnp.concatenate(anchor_values + [kv_ref[1]], 0)
    row = lax.broadcasted_iota(jnp.int32, (BLOCK, 2 * BLOCK), 0)
    column = lax.broadcasted_iota(jnp.int32, (BLOCK, 2 * BLOCK), 1)
    allowed = (column >= filler) & (column <= row + BLOCK)
    for j in range(GROUP):
        lanes = slice(j * D, (j + 1) * D)
        scores = jnp.where(allowed, dot_nt(q_ref[:, lanes], keys), FILLER)
        highest = jnp.max(scores, 1, keepdims=True)
        weights = jnp.exp2((scores - highest) * SCALE)
        total = jnp.sum(weights, 1, keepdims=True)
        out_ref[:, lanes] = (dot_nn(weights.astype(BF16), values) / total).astype(BF16)

    diagonal = (
        lax.broadcasted_iota(jnp.int32, (QROWS, D), 0) == lax.broadcasted_iota(jnp.int32, (QROWS, D), 1)
    )
    logs = []
    for y in range(QUARTERS):
        parts = in_ref[y * KV_HEADS + head, B_S:B_ROWS, :].astype(F32)
        logs.append(parts[0:1, :] + parts[1:2, :] + parts[2:3, :])
    highest = functools.reduce(jnp.maximum, logs)
    shares = [jnp.exp2(log - highest) for log in logs]
    whole = functools.reduce(jnp.add, shares)
    merged = jnp.zeros((QROWS, D), F32)
    for y in range(QUARTERS):
        share = jnp.sum(jnp.where(diagonal, shares[y] / whole, 0.0), 1, keepdims=True)
        partial = (
            in_ref[y * KV_HEADS + head, B_HI:B_HI + QROWS, :].astype(F32)
            + in_ref[y * KV_HEADS + head, B_LO:B_LO + QROWS, :].astype(F32)
        )
        merged = merged + share * partial
    for j in range(GROUP):
        query_out_ref[:, j * D:(j + 1) * D] = merged[j * ROWS:(j + 1) * ROWS, :].astype(BF16)


VMEM = pl.BlockSpec(memory_space=pltpu.VMEM)
SMEM = pl.BlockSpec(memory_space=pltpu.SMEM)
PARAMS = pltpu.CompilerParams(vmem_limit_bytes=40 * 1024 * 1024)


def per_device(context_q, context_key_value, query_token_queries, query_key_value):
    place = lax.axis_index("ctx").astype(jnp.int32).reshape(1)
    packed = pl.pallas_call(
        pack_kernel,
        out_shape=jax.ShapeDtypeStruct((CTX, A_ROWS, D), BF16),
        in_specs=[VMEM, VMEM, VMEM],
        out_specs=VMEM,
        compiler_params=PARAMS,
    )(context_key_value, query_token_queries, query_key_value)
    received = lax.all_to_all(packed, "ctx", 0, 0)
    partial = pl.pallas_call(
        query_kernel,
        out_shape=jax.ShapeDtypeStruct((CTX, B_ROWS, D), BF16),
        in_specs=[SMEM, VMEM],
        out_specs=VMEM,
        compiler_params=PARAMS,
    )(place, received)
    gathered = lax.all_to_all(partial, "ctx", 0, 0)
    width = GROUP * D
    return pl.pallas_call(
        encode_kernel,
        grid=(KV_HEADS,),
        out_shape=(
            jax.ShapeDtypeStruct(context_q.shape, BF16),
            jax.ShapeDtypeStruct(query_token_queries.shape, BF16),
        ),
        in_specs=[
            SMEM,
            pl.BlockSpec((BLOCK, width), lambda h: (0, h)),
            pl.BlockSpec((2, BLOCK, D), lambda h: (0, 0, h)),
            VMEM,
        ],
        out_specs=(
            pl.BlockSpec((BLOCK, width), lambda h: (0, h)),
            pl.BlockSpec((ROWS, width), lambda h: (0, h)),
        ),
        compiler_params=PARAMS,
    )(place, context_q, context_key_value, gathered)


def solution(mesh):
    return jax.shard_map(
        per_device,
        mesh=mesh,
        in_specs=(
            P(("req", "ctx"), None),
            P(None, ("req", "ctx"), None),
            P(("req", "ctx"), None),
            P(None, ("req", "ctx"), None),
        ),
        out_specs=(P(("req", "ctx"), None), P(("req", "ctx"), None)),
        check_vma=False,
    )
```

```python
import functools

import jax
import jax.numpy as jnp
from jax import lax
from jax.experimental import pallas as pl
from jax.experimental.pallas import tpu as pltpu
from jax.sharding import PartitionSpec as P

KV_HEADS = 8
GROUP = 8
D = 128
BLOCK = 128
QUARTERS = 4
CTX = QUARTERS * KV_HEADS
PIECE = BLOCK // QUARTERS
ROWS = 4
QROWS = ROWS * GROUP
F32 = jnp.float32
BF16 = jnp.bfloat16
FILLER = -1e30
LOG2E = 1.4426950408889634
SCALE = D ** -0.5 * LOG2E

A_K, A_V, A_Q, A_S = 0, PIECE, 2 * PIECE, 2 * PIECE + QROWS
A_ROWS = A_S + 8
B_S = QROWS
B_ROWS = B_S + 8


def dot_nt(a, b):
    return lax.dot_general(a, b, (((1,), (1,)), ((), ())), preferred_element_type=F32)


def dot_nn(a, b):
    return lax.dot_general(a, b, (((1,), (0,)), ((), ())), preferred_element_type=F32)


def pack_kernel(kv_hbm, q_hbm, qkv_hbm, out_ref, kv_ref, q_ref, qkv_ref, sems):
    copies = [
        pltpu.make_async_copy(source, target, sems.at[i])
        for i, (source, target) in enumerate(((q_hbm, q_ref), (qkv_hbm, qkv_ref), (kv_hbm, kv_ref)))
    ]
    for copy in copies:
        copy.start()
    for copy in copies:
        copy.wait()
    q = q_ref[...].astype(F32)
    qkv = qkv_ref[...].astype(F32)
    for head in range(KV_HEADS):
        lanes = slice(head * D, (head + 1) * D)
        first = head * GROUP * D
        queries = jnp.concatenate(
            [q[:, first + j * D:first + (j + 1) * D] for j in range(GROUP)], 0
        ).astype(BF16)
        for quarter in range(QUARTERS):
            dest = quarter * KV_HEADS + head
            rows = slice(quarter * PIECE, (quarter + 1) * PIECE)
            out_ref[dest, A_K:A_K + PIECE, :] = kv_ref[0, rows, lanes]
            out_ref[dest, A_V:A_V + PIECE, :] = kv_ref[1, rows, lanes]
            out_ref[dest, A_Q:A_Q + QROWS, :] = queries
            out_ref[dest, A_S:A_ROWS, :] = jnp.concatenate(
                [qkv[0, quarter:quarter + 1, lanes], qkv[1, quarter:quarter + 1, lanes], jnp.zeros((6, D), F32)], 0
            ).astype(BF16)


CHUNK = 8
STACK = 4


def query_kernel(place_ref, in_ref, out_ref):
    quarter = place_ref[0] // KV_HEADS
    keys = in_ref[:, A_K:A_K + PIECE, :].reshape(CTX * PIECE, D)
    values = in_ref[:, A_V:A_V + PIECE, :].reshape(CTX * PIECE, D)
    tail = in_ref[:, A_S:A_ROWS, :].astype(F32)
    self_keys = tail[:, 0, :].astype(BF16)
    self_values = tail[:, 1, :].astype(BF16)
    rows = CHUNK * QROWS
    row_id = lax.broadcasted_iota(jnp.int32, (rows, CTX), 0)
    key_pos = lax.broadcasted_iota(jnp.int32, (rows, CTX), 1) * ROWS + quarter
    row_pos = (row_id // QROWS) * ROWS + row_id % ROWS
    diagonal = (
        lax.broadcasted_iota(jnp.int32, (CHUNK, QROWS, D), 1)
        == lax.broadcasted_iota(jnp.int32, (CHUNK, QROWS, D), 2)
    )
    for chunk in range(CTX // CHUNK):
        sources = slice(chunk * CHUNK, (chunk + 1) * CHUNK)
        queries = in_ref[sources, A_Q:A_Q + QROWS, :].reshape(rows, D)
        scores = dot_nt(queries, keys)
        self_scores = dot_nt(queries, self_keys)
        self_scores = jnp.where(key_pos <= row_pos + chunk * CHUNK * ROWS, self_scores, FILLER)
        highest = jnp.maximum(jnp.max(scores, 1, keepdims=True), jnp.max(self_scores, 1, keepdims=True))
        weights = jnp.exp2((scores - highest) * SCALE)
        self_weights = jnp.exp2((self_scores - highest) * SCALE)
        total = jnp.sum(weights, 1, keepdims=True) + jnp.sum(self_weights, 1, keepdims=True)
        summed = dot_nn(weights.astype(BF16), values) + dot_nn(self_weights.astype(BF16), self_values)
        partial = (summed / total).reshape(CHUNK, QROWS, D)
        out_ref[sources, 0:QROWS, :] = partial
        log_sum = (highest * SCALE + jnp.log2(total)).reshape(CHUNK, QROWS, 1)
        log_row = jnp.sum(jnp.where(diagonal, log_sum, 0.0), 1, keepdims=True)
        first = log_row.astype(BF16).astype(F32)
        second = (log_row - first).astype(BF16).astype(F32)
        third = log_row - first - second
        out_ref[sources, B_S:B_ROWS, :] = jnp.concatenate(
            [first, second, third, jnp.zeros((CHUNK, 5, D), F32)], 1
        )


def encode_kernel(
    place_ref, q_hbm, kv_hbm, a0_hbm, a1_hbm, a2_hbm, a3_hbm, out_hbm, q_ref, kv_ref, out_ref, q_sems, kv_sems, sems
):
    width = GROUP * D

    def copy_in(head):
        lanes = pl.ds(pl.multiple_of(head * width, width), width)
        return pltpu.make_async_copy(q_hbm.at[:, lanes], q_ref.at[:, lanes], q_sems.at[head])

    def copy_out(head):
        lanes = pl.ds(pl.multiple_of(head * width, width), width)
        return pltpu.make_async_copy(out_ref.at[:, lanes], out_hbm.at[:, lanes], sems.at[head])

    copies = [
        pltpu.make_async_copy(source, kv_ref.at[:, PIECE * i:PIECE * i + source.shape[1], :], kv_sems.at[i])
        for i, source in enumerate((a0_hbm, a1_hbm, a2_hbm, a3_hbm, kv_hbm))
    ]
    for copy in copies:
        copy.start()
    for head in range(KV_HEADS):
        copy_in(head).start()
    filler = jnp.where(place_ref[0] > 0, 0, BLOCK)
    row = lax.broadcasted_iota(jnp.int32, (BLOCK, 2 * BLOCK), 0)
    column = lax.broadcasted_iota(jnp.int32, (BLOCK, 2 * BLOCK), 1)
    allowed = (column >= filler) & (column <= row + BLOCK)
    for copy in copies:
        copy.wait()

    def one_head(head, carry):
        copy_in(head).wait()
        kv_lanes = pl.ds(pl.multiple_of(head * D, D), D)
        keys = kv_ref[0, :, kv_lanes]
        values = kv_ref[1, :, kv_lanes]
        for first in range(0, GROUP, STACK):
            lanes = [pl.ds(pl.multiple_of(head * width + (first + j) * D, D), D) for j in range(STACK)]
            queries = jnp.concatenate([q_ref[:, each] for each in lanes], 0)
            scores = dot_nt(queries, keys).reshape(STACK, BLOCK, 2 * BLOCK)
            scores = jnp.where(allowed[None], scores, FILLER)
            highest = jnp.max(scores, 2, keepdims=True)
            weights = jnp.exp2((scores - highest) * SCALE)
            total = jnp.sum(weights, 2, keepdims=True)
            summed = dot_nn(weights.astype(BF16).reshape(STACK * BLOCK, 2 * BLOCK), values)
            attended = (summed.reshape(STACK, BLOCK, D) / total).astype(BF16)
            for j in range(STACK):
                out_ref[:, lanes[j]] = attended[j]
        copy_out(head).start()
        return carry

    lax.fori_loop(0, KV_HEADS, one_head, 0)
    for head in range(KV_HEADS):
        copy_out(head).wait()


def merge_kernel(in_ref, out_ref):
    diagonal = (
        lax.broadcasted_iota(jnp.int32, (KV_HEADS, QROWS, D), 1)
        == lax.broadcasted_iota(jnp.int32, (KV_HEADS, QROWS, D), 2)
    )
    logs = []
    for y in range(QUARTERS):
        parts = in_ref[y * KV_HEADS:(y + 1) * KV_HEADS, B_S:B_ROWS, :]
        logs.append(parts[:, 0:1, :] + parts[:, 1:2, :] + parts[:, 2:3, :])
    highest = functools.reduce(jnp.maximum, logs)
    shares = [jnp.exp2(log - highest) for log in logs]
    whole = functools.reduce(jnp.add, shares)
    merged = jnp.zeros((KV_HEADS, QROWS, D), F32)
    for y in range(QUARTERS):
        share = jnp.sum(jnp.where(diagonal, shares[y] / whole, 0.0), 2, keepdims=True)
        sources = slice(y * KV_HEADS, (y + 1) * KV_HEADS)
        merged = merged + share * in_ref[sources, 0:QROWS, :]
    for head in range(KV_HEADS):
        for j in range(GROUP):
            first = (head * GROUP + j) * D
            out_ref[:, first:first + D] = merged[head, j * ROWS:(j + 1) * ROWS, :].astype(BF16)


VMEM = pl.BlockSpec(memory_space=pltpu.VMEM)
ANY = pl.BlockSpec(memory_space=pl.ANY)
SMEM = pl.BlockSpec(memory_space=pltpu.SMEM)
HBM = pl.BlockSpec(memory_space=pltpu.HBM)
PARAMS = pltpu.CompilerParams(vmem_limit_bytes=32 * 1024 * 1024)


def cost(flops, nbytes):
    return pl.CostEstimate(flops=flops, bytes_accessed=nbytes, transcendentals=0)


def at(quarter, z):
    return quarter * KV_HEADS + z


def scatter_anchor(kv):
    quarters = [kv[:, q * PIECE:(q + 1) * PIECE, :] for q in range(QUARTERS)]
    mine = jnp.where(lax.axis_index("ctx") == 0, quarters[0], 0)
    for q in range(1, QUARTERS):
        mine = mine + lax.ppermute(quarters[q], "ctx", [(0, at(q, 0))])
    return mine


def fan_along_z(mine):
    root = mine
    for step in (4, 2, 6):
        mine = mine + lax.ppermute(root, "ctx", [(at(y, 0), at(y, step)) for y in range(QUARTERS)])
    return mine


def pair_along_z(mine):
    pairs = [(at(y, z), at(y, z + 1)) for y in range(QUARTERS) for z in range(0, KV_HEADS, 2)]
    return mine + lax.ppermute(mine, "ctx", pairs)


def gather_along_y(mine):
    devices = [(y, z) for y in range(QUARTERS) for z in range(KV_HEADS)]
    return [mine] + [
        lax.ppermute(mine, "ctx", [(at(y, z), at((y + k) % QUARTERS, z)) for y, z in devices])
        for k in range(1, QUARTERS)
    ]


def per_device(context_q, context_key_value, query_token_queries, query_key_value):
    place = lax.axis_index("ctx").astype(jnp.int32).reshape(1)
    packed = pl.pallas_call(
        pack_kernel,
        out_shape=jax.ShapeDtypeStruct((CTX, A_ROWS, D), BF16),
        in_specs=[HBM, HBM, HBM],
        out_specs=VMEM,
        scratch_shapes=[
            pltpu.VMEM(context_key_value.shape, BF16),
            pltpu.VMEM(query_token_queries.shape, BF16),
            pltpu.VMEM(query_key_value.shape, BF16),
            pltpu.SemaphoreType.DMA((3,)),
        ],
        compiler_params=pltpu.CompilerParams(vmem_limit_bytes=60 * 1024 * 1024),
        cost_estimate=cost(0, 1 << 21),
    )(context_key_value, query_token_queries, query_key_value)
    quarter = scatter_anchor(context_key_value)
    received = lax.all_to_all(packed, "ctx", 0, 0)
    quarter = fan_along_z(quarter)
    received, quarter = lax.optimization_barrier((received, quarter))
    quarter = pair_along_z(quarter)
    partial = pl.pallas_call(
        query_kernel,
        out_shape=jax.ShapeDtypeStruct((CTX, B_ROWS, D), F32),
        in_specs=[SMEM, VMEM],
        out_specs=VMEM,
        compiler_params=PARAMS,
        cost_estimate=cost(1 << 29, 1 << 21),
    )(place, received)
    partial, quarter = lax.optimization_barrier((partial, quarter))
    anchor = gather_along_y(quarter)
    gathered = lax.all_to_all(partial.astype(jnp.float16), "ctx", 0, 0).astype(F32)
    context_out = pl.pallas_call(
        encode_kernel,
        out_shape=jax.ShapeDtypeStruct(context_q.shape, BF16),
        in_specs=[SMEM, HBM, HBM] + [ANY] * QUARTERS,
        out_specs=HBM,
        scratch_shapes=[
            pltpu.VMEM(context_q.shape, BF16),
            pltpu.VMEM((2, 2 * BLOCK, KV_HEADS * D), BF16),
            pltpu.VMEM(context_q.shape, BF16),
            pltpu.SemaphoreType.DMA((KV_HEADS,)),
            pltpu.SemaphoreType.DMA((QUARTERS + 1,)),
            pltpu.SemaphoreType.DMA((KV_HEADS,)),
        ],
        compiler_params=pltpu.CompilerParams(vmem_limit_bytes=56 * 1024 * 1024),
        cost_estimate=cost(1 << 36, 1 << 24),
    )(place, context_q, context_key_value, *anchor)
    query_out = pl.pallas_call(
        merge_kernel,
        out_shape=jax.ShapeDtypeStruct(query_token_queries.shape, BF16),
        in_specs=[VMEM],
        out_specs=VMEM,
        compiler_params=PARAMS,
        cost_estimate=cost(1 << 20, 1 << 20),
    )(gathered)
    return context_out, query_out


def solution(mesh):
    return jax.shard_map(
        per_device,
        mesh=mesh,
        in_specs=(
            P(("req", "ctx"), None),
            P(None, ("req", "ctx"), None),
            P(("req", "ctx"), None),
            P(None, ("req", "ctx"), None),
        ),
        out_specs=(P(("req", "ctx"), None), P(("req", "ctx"), None)),
        check_vma=False,
    )
```

```python
import functools

import jax
import jax.numpy as jnp
from jax import lax
from jax.experimental import pallas as pl
from jax.experimental.pallas import tpu as pltpu
from jax.sharding import PartitionSpec as P

KV_HEADS = 8
GROUP = 8
D = 128
BLOCK = 128
QUARTERS = 4
CTX = QUARTERS * KV_HEADS
PIECE = BLOCK // QUARTERS
ROWS = 4
QROWS = ROWS * GROUP
F32 = jnp.float32
BF16 = jnp.bfloat16
FILLER = -1e30
LOG2E = 1.4426950408889634
SCALE = D ** -0.5 * LOG2E

A_K, A_V, A_Q, A_S = 0, PIECE, 2 * PIECE, 2 * PIECE + QROWS
A_ROWS = A_S + 8
B_S = QROWS
B_ROWS = B_S + 8


def dot_nt(a, b):
    return lax.dot_general(a, b, (((1,), (1,)), ((), ())), preferred_element_type=F32)


def dot_nn(a, b):
    return lax.dot_general(a, b, (((1,), (0,)), ((), ())), preferred_element_type=F32)


def pack_kernel(kv_hbm, q_hbm, qkv_hbm, out_ref, kv_ref, q_ref, qkv_ref, sems):
    copies = [
        pltpu.make_async_copy(source, target, sems.at[i])
        for i, (source, target) in enumerate(((q_hbm, q_ref), (qkv_hbm, qkv_ref), (kv_hbm, kv_ref)))
    ]
    for copy in copies:
        copy.start()
    for copy in copies:
        copy.wait()
    q = q_ref[...].astype(F32)
    qkv = qkv_ref[...].astype(F32)
    for head in range(KV_HEADS):
        lanes = slice(head * D, (head + 1) * D)
        first = head * GROUP * D
        queries = jnp.concatenate(
            [q[:, first + j * D:first + (j + 1) * D] for j in range(GROUP)], 0
        ).astype(BF16)
        for quarter in range(QUARTERS):
            dest = quarter * KV_HEADS + head
            rows = slice(quarter * PIECE, (quarter + 1) * PIECE)
            out_ref[dest, A_K:A_K + PIECE, :] = kv_ref[0, rows, lanes]
            out_ref[dest, A_V:A_V + PIECE, :] = kv_ref[1, rows, lanes]
            out_ref[dest, A_Q:A_Q + QROWS, :] = queries
            out_ref[dest, A_S:A_ROWS, :] = jnp.concatenate(
                [qkv[0, quarter:quarter + 1, lanes], qkv[1, quarter:quarter + 1, lanes], jnp.zeros((6, D), F32)], 0
            ).astype(BF16)


CHUNK = 8
STACK = 4


def query_kernel(place_ref, in_ref, out_ref):
    quarter = place_ref[0] // KV_HEADS
    keys = in_ref[:, A_K:A_K + PIECE, :].reshape(CTX * PIECE, D)
    values = in_ref[:, A_V:A_V + PIECE, :].reshape(CTX * PIECE, D)
    tail = in_ref[:, A_S:A_ROWS, :].astype(F32)
    self_keys = tail[:, 0, :].astype(BF16)
    self_values = tail[:, 1, :].astype(BF16)
    rows = CHUNK * QROWS
    row_id = lax.broadcasted_iota(jnp.int32, (rows, CTX), 0)
    key_pos = lax.broadcasted_iota(jnp.int32, (rows, CTX), 1) * ROWS + quarter
    row_pos = (row_id // QROWS) * ROWS + row_id % ROWS
    diagonal = (
        lax.broadcasted_iota(jnp.int32, (CHUNK, QROWS, D), 1)
        == lax.broadcasted_iota(jnp.int32, (CHUNK, QROWS, D), 2)
    )
    for chunk in range(CTX // CHUNK):
        sources = slice(chunk * CHUNK, (chunk + 1) * CHUNK)
        queries = in_ref[sources, A_Q:A_Q + QROWS, :].reshape(rows, D)
        scores = dot_nt(queries, keys)
        self_scores = dot_nt(queries, self_keys)
        self_scores = jnp.where(key_pos <= row_pos + chunk * CHUNK * ROWS, self_scores, FILLER)
        highest = jnp.maximum(jnp.max(scores, 1, keepdims=True), jnp.max(self_scores, 1, keepdims=True))
        weights = jnp.exp2((scores - highest) * SCALE)
        self_weights = jnp.exp2((self_scores - highest) * SCALE)
        total = jnp.sum(weights, 1, keepdims=True) + jnp.sum(self_weights, 1, keepdims=True)
        summed = dot_nn(weights.astype(BF16), values) + dot_nn(self_weights.astype(BF16), self_values)
        partial = (summed / total).reshape(CHUNK, QROWS, D)
        out_ref[sources, 0:QROWS, :] = partial
        log_sum = (highest * SCALE + jnp.log2(total)).reshape(CHUNK, QROWS, 1)
        log_row = jnp.sum(jnp.where(diagonal, log_sum, 0.0), 1, keepdims=True)
        first = log_row.astype(BF16).astype(F32)
        second = (log_row - first).astype(BF16).astype(F32)
        third = log_row - first - second
        out_ref[sources, B_S:B_ROWS, :] = jnp.concatenate(
            [first, second, third, jnp.zeros((CHUNK, 5, D), F32)], 1
        )


def encode_kernel(
    place_ref, q_hbm, kv_hbm, a0_hbm, a1_hbm, a2_hbm, a3_hbm, out_hbm, q_ref, kv_ref, out_ref, q_sems, kv_sems, sems
):
    width = GROUP * D

    def copy_in(head):
        lanes = pl.ds(pl.multiple_of(head * width, width), width)
        return pltpu.make_async_copy(q_hbm.at[:, lanes], q_ref.at[:, lanes], q_sems.at[head])

    def copy_out(head):
        lanes = pl.ds(pl.multiple_of(head * width, width), width)
        return pltpu.make_async_copy(out_ref.at[:, lanes], out_hbm.at[:, lanes], sems.at[head])

    copies = [
        pltpu.make_async_copy(source, kv_ref.at[:, PIECE * i:PIECE * i + source.shape[1], :], kv_sems.at[i])
        for i, source in enumerate((a0_hbm, a1_hbm, a2_hbm, a3_hbm, kv_hbm))
    ]
    for copy in copies:
        copy.start()
    for head in range(KV_HEADS):
        copy_in(head).start()
    filler = jnp.where(place_ref[0] > 0, 0, BLOCK)
    row = lax.broadcasted_iota(jnp.int32, (BLOCK, 2 * BLOCK), 0)
    column = lax.broadcasted_iota(jnp.int32, (BLOCK, 2 * BLOCK), 1)
    allowed = (column >= filler) & (column <= row + BLOCK)
    for copy in copies:
        copy.wait()

    def one_head(head, carry):
        copy_in(head).wait()
        kv_lanes = pl.ds(pl.multiple_of(head * D, D), D)
        keys = kv_ref[0, :, kv_lanes]
        values = kv_ref[1, :, kv_lanes]
        for first in range(0, GROUP, STACK):
            lanes = [pl.ds(pl.multiple_of(head * width + (first + j) * D, D), D) for j in range(STACK)]
            queries = jnp.concatenate([q_ref[:, each] for each in lanes], 0)
            scores = dot_nt(queries, keys).reshape(STACK, BLOCK, 2 * BLOCK)
            scores = jnp.where(allowed[None], scores, FILLER)
            highest = jnp.max(scores, 2, keepdims=True)
            weights = jnp.exp2((scores - highest) * SCALE)
            total = jnp.sum(weights, 2, keepdims=True)
            summed = dot_nn(weights.astype(BF16).reshape(STACK * BLOCK, 2 * BLOCK), values)
            attended = (summed.reshape(STACK, BLOCK, D) / total).astype(BF16)
            for j in range(STACK):
                out_ref[:, lanes[j]] = attended[j]
        copy_out(head).start()
        return carry

    lax.fori_loop(0, KV_HEADS, one_head, 0)
    for head in range(KV_HEADS):
        copy_out(head).wait()


def merge_kernel(in_ref, out_ref):
    diagonal = (
        lax.broadcasted_iota(jnp.int32, (KV_HEADS, QROWS, D), 1)
        == lax.broadcasted_iota(jnp.int32, (KV_HEADS, QROWS, D), 2)
    )
    logs = []
    for y in range(QUARTERS):
        parts = in_ref[y * KV_HEADS:(y + 1) * KV_HEADS, B_S:B_ROWS, :]
        logs.append(parts[:, 0:1, :] + parts[:, 1:2, :] + parts[:, 2:3, :])
    highest = functools.reduce(jnp.maximum, logs)
    shares = [jnp.exp2(log - highest) for log in logs]
    whole = functools.reduce(jnp.add, shares)
    merged = jnp.zeros((KV_HEADS, QROWS, D), F32)
    for y in range(QUARTERS):
        share = jnp.sum(jnp.where(diagonal, shares[y] / whole, 0.0), 2, keepdims=True)
        sources = slice(y * KV_HEADS, (y + 1) * KV_HEADS)
        merged = merged + share * in_ref[sources, 0:QROWS, :]
    for head in range(KV_HEADS):
        for j in range(GROUP):
            first = (head * GROUP + j) * D
            out_ref[:, first:first + D] = merged[head, j * ROWS:(j + 1) * ROWS, :].astype(BF16)


VMEM = pl.BlockSpec(memory_space=pltpu.VMEM)
ANY = pl.BlockSpec(memory_space=pl.ANY)
SMEM = pl.BlockSpec(memory_space=pltpu.SMEM)
HBM = pl.BlockSpec(memory_space=pltpu.HBM)
PARAMS = pltpu.CompilerParams(vmem_limit_bytes=32 * 1024 * 1024)


def cost(flops, nbytes):
    return pl.CostEstimate(flops=flops, bytes_accessed=nbytes, transcendentals=0)


def at(quarter, z):
    return quarter * KV_HEADS + z


def scatter_anchor(kv):
    quarters = [kv[:, q * PIECE:(q + 1) * PIECE, :] for q in range(QUARTERS)]
    mine = jnp.where(lax.axis_index("ctx") == 0, quarters[0], 0)
    for q in range(1, QUARTERS):
        mine = mine + lax.ppermute(quarters[q], "ctx", [(0, at(q, 0))])
    return mine


FAN = (2, 6, 5)


def fan_along_z(mine):
    root = mine
    for step in FAN:
        mine = mine + lax.ppermute(root, "ctx", [(at(y, 0), at(y, step)) for y in range(QUARTERS)])
    return mine


def pair_along_z(mine):
    pairs = [(at(y, z), at(y, z ^ 1)) for y in range(QUARTERS) for z in (0,) + FAN]
    return lax.ppermute(mine, "ctx", pairs)


def gather_along_y(mine):
    devices = [(y, z) for y in range(QUARTERS) for z in range(KV_HEADS)]
    return [mine] + [
        lax.ppermute(mine, "ctx", [(at(y, z), at((y + k) % QUARTERS, z)) for y, z in devices])
        for k in range(1, QUARTERS)
    ]


def per_device(context_q, context_key_value, query_token_queries, query_key_value):
    place = lax.axis_index("ctx").astype(jnp.int32).reshape(1)
    packed = pl.pallas_call(
        pack_kernel,
        out_shape=jax.ShapeDtypeStruct((CTX, A_ROWS, D), BF16),
        in_specs=[HBM, HBM, HBM],
        out_specs=VMEM,
        scratch_shapes=[
            pltpu.VMEM(context_key_value.shape, BF16),
            pltpu.VMEM(query_token_queries.shape, BF16),
            pltpu.VMEM(query_key_value.shape, BF16),
            pltpu.SemaphoreType.DMA((3,)),
        ],
        compiler_params=pltpu.CompilerParams(vmem_limit_bytes=60 * 1024 * 1024),
        cost_estimate=cost(0, 1 << 21),
    )(context_key_value, query_token_queries, query_key_value)
    quarter = scatter_anchor(context_key_value)
    received = lax.all_to_all(packed, "ctx", 0, 0)
    quarter = fan_along_z(quarter)
    from_pair = pair_along_z(quarter)
    received, quarter = lax.optimization_barrier((received, quarter))
    quarter = quarter + from_pair
    partial = pl.pallas_call(
        query_kernel,
        out_shape=jax.ShapeDtypeStruct((CTX, B_ROWS, D), F32),
        in_specs=[SMEM, VMEM],
        out_specs=VMEM,
        compiler_params=PARAMS,
        cost_estimate=cost(1 << 29, 1 << 21),
    )(place, received)
    partial, quarter = lax.optimization_barrier((partial, quarter))
    anchor = gather_along_y(quarter)
    gathered = lax.all_to_all(partial.astype(jnp.float16), "ctx", 0, 0).astype(F32)
    context_out = pl.pallas_call(
        encode_kernel,
        out_shape=jax.ShapeDtypeStruct(context_q.shape, BF16),
        in_specs=[SMEM, HBM, HBM] + [VMEM] * QUARTERS,
        out_specs=HBM,
        scratch_shapes=[
            pltpu.VMEM(context_q.shape, BF16),
            pltpu.VMEM((2, 2 * BLOCK, KV_HEADS * D), BF16),
            pltpu.VMEM(context_q.shape, BF16),
            pltpu.SemaphoreType.DMA((KV_HEADS,)),
            pltpu.SemaphoreType.DMA((QUARTERS + 1,)),
            pltpu.SemaphoreType.DMA((KV_HEADS,)),
        ],
        compiler_params=pltpu.CompilerParams(vmem_limit_bytes=52 * 1024 * 1024),
        cost_estimate=cost(1 << 36, 1 << 24),
    )(place, context_q, context_key_value, *anchor)
    query_out = pl.pallas_call(
        merge_kernel,
        out_shape=jax.ShapeDtypeStruct(query_token_queries.shape, BF16),
        in_specs=[VMEM],
        out_specs=VMEM,
        compiler_params=PARAMS,
        cost_estimate=cost(1 << 20, 1 << 20),
    )(gathered)
    return context_out, query_out


def solution(mesh):
    return jax.shard_map(
        per_device,
        mesh=mesh,
        in_specs=(
            P(("req", "ctx"), None),
            P(None, ("req", "ctx"), None),
            P(("req", "ctx"), None),
            P(None, ("req", "ctx"), None),
        ),
        out_specs=(P(("req", "ctx"), None), P(("req", "ctx"), None)),
        check_vma=False,
    )
```

```python
import functools

import jax
import jax.numpy as jnp
from jax import lax
from jax.experimental import pallas as pl
from jax.experimental.pallas import tpu as pltpu
from jax.sharding import PartitionSpec as P

KV_HEADS = 8
GROUP = 8
D = 128
BLOCK = 128
YS = 4
PAIRS = 4
SIDES = 2
CTX = YS * PAIRS * SIDES
ROWS = 4
QROWS = ROWS * GROUP
F32 = jnp.float32
BF16 = jnp.bfloat16
FILLER = -1e30
LOG2E = 1.4426950408889634
SCALE = D ** -0.5 * LOG2E

STEPS = [(dy, flip) for dy in range(YS) for flip in range(SIDES)]
A_K, A_V, A_SK, A_SV = 0, BLOCK, 2 * BLOCK, 2 * BLOCK + 8
A_ROWS = A_SV + 8
B_S = QROWS
B_ROWS = B_S + 8


def dot_nt(a, b):
    return lax.dot_general(a, b, (((1,), (1,)), ((), ())), preferred_element_type=F32)


def dot_nn(a, b):
    return lax.dot_general(a, b, (((1,), (0,)), ((), ())), preferred_element_type=F32)


def pack_kernel(place_ref, kv_hbm, q_hbm, qkv_hbm, *refs):
    kv_out_refs, (q_out_ref, kv_ref, q_ref, qkv_ref, sems) = refs[:KV_HEADS], refs[KV_HEADS:]
    copies = [
        pltpu.make_async_copy(source, target, sems.at[i])
        for i, (source, target) in enumerate(((q_hbm, q_ref), (qkv_hbm, qkv_ref), (kv_hbm, kv_ref)))
    ]
    for copy in copies:
        copy.start()
    for copy in copies:
        copy.wait()
    q = q_ref[...].astype(F32)
    for head in range(KV_HEADS):
        first = head * GROUP * D
        queries = jnp.concatenate(
            [q[:, first + j * D:first + (j + 1) * D] for j in range(GROUP)], 0
        ).astype(BF16)
        for pair in range(PAIRS):
            q_out_ref[head // SIDES * PAIRS * SIDES + pair * SIDES + head % SIDES] = queries
    y, side = place_ref[0] // (PAIRS * SIDES), place_ref[0] % SIDES
    blank = jnp.zeros((8 - ROWS, D), F32)
    for (dy, flip), out_ref in zip(STEPS, kv_out_refs):
        head = (y + dy) % YS * SIDES + (side + flip) % SIDES
        lanes = pl.ds(pl.multiple_of(head * D, D), D)
        out_ref[A_K:A_K + BLOCK, :] = kv_ref[0, :, lanes]
        out_ref[A_V:A_V + BLOCK, :] = kv_ref[1, :, lanes]
        out_ref[A_SK:A_ROWS, :] = jnp.concatenate(
            [qkv_ref[0, :, lanes].astype(F32), blank, qkv_ref[1, :, lanes].astype(F32), blank], 0
        ).astype(BF16)


CHUNK = 8
STACK = 4


def query_kernel(place_ref, *refs):
    kv_refs, (q_ref, out_ref) = refs[:KV_HEADS], refs[KV_HEADS:]
    place = place_ref[0]
    y, pair, side = place // (PAIRS * SIDES), place // SIDES % PAIRS, place % SIDES
    keys = jnp.concatenate([ref[A_K:A_K + BLOCK, :] for ref in kv_refs], 0)
    values = jnp.concatenate([ref[A_V:A_V + BLOCK, :] for ref in kv_refs], 0)
    tails = [ref[A_SK:A_ROWS, :].astype(F32) for ref in kv_refs]
    self_keys = jnp.concatenate([tail[0:8] for tail in tails], 0).astype(BF16)
    self_values = jnp.concatenate([tail[8:16] for tail in tails], 0).astype(BF16)
    rows = CHUNK * QROWS
    row_id = lax.broadcasted_iota(jnp.int32, (rows, KV_HEADS * 8), 0)
    column = lax.broadcasted_iota(jnp.int32, (rows, KV_HEADS * 8), 1)
    source, key_row = column // 8, column % 8
    source_y, source_side = (y + YS - source // SIDES) % YS, (side + source % SIDES) % SIDES
    key_pos = (source_y * (PAIRS * SIDES) + pair * SIDES + source_side) * ROWS + key_row
    key_pos = jnp.where(key_row < ROWS, key_pos, CTX * ROWS)
    row_pos = (row_id // QROWS) * ROWS + row_id % ROWS
    diagonal = (
        lax.broadcasted_iota(jnp.int32, (CHUNK, QROWS, D), 1)
        == lax.broadcasted_iota(jnp.int32, (CHUNK, QROWS, D), 2)
    )
    for chunk in range(CTX // CHUNK):
        sources = slice(chunk * CHUNK, (chunk + 1) * CHUNK)
        queries = q_ref[sources].reshape(rows, D)
        scores = dot_nt(queries, keys)
        self_scores = dot_nt(queries, self_keys)
        self_scores = jnp.where(key_pos <= row_pos + chunk * CHUNK * ROWS, self_scores, FILLER)
        highest = jnp.maximum(jnp.max(scores, 1, keepdims=True), jnp.max(self_scores, 1, keepdims=True))
        weights = jnp.exp2((scores - highest) * SCALE)
        self_weights = jnp.exp2((self_scores - highest) * SCALE)
        total = jnp.sum(weights, 1, keepdims=True) + jnp.sum(self_weights, 1, keepdims=True)
        summed = dot_nn(weights.astype(BF16), values) + dot_nn(self_weights.astype(BF16), self_values)
        out_ref[sources, 0:QROWS, :] = (summed / total).reshape(CHUNK, QROWS, D)
        log_sum = (highest * SCALE + jnp.log2(total)).reshape(CHUNK, QROWS, 1)
        log_row = jnp.sum(jnp.where(diagonal, log_sum, 0.0), 1, keepdims=True)
        first = log_row.astype(BF16).astype(F32)
        second = (log_row - first).astype(BF16).astype(F32)
        third = log_row - first - second
        out_ref[sources, B_S:B_ROWS, :] = jnp.concatenate(
            [first, second, third, jnp.zeros((CHUNK, 5, D), F32)], 1
        )


def encode_kernel(
    place_ref, q_hbm, kv_hbm, a0_ref, a1_ref, a2_ref, a3_ref, out_hbm,
    q_ref, kv_ref, anchor_ref, out_ref, q_sems, kv_sems, sems
):
    width = GROUP * D
    y = place_ref[0] // (PAIRS * SIDES)

    def copy_in(head):
        lanes = pl.ds(pl.multiple_of(head * width, width), width)
        return pltpu.make_async_copy(q_hbm.at[:, lanes], q_ref.at[:, lanes], q_sems.at[head])

    def copy_out(head):
        lanes = pl.ds(pl.multiple_of(head * width, width), width)
        return pltpu.make_async_copy(out_ref.at[:, lanes], out_hbm.at[:, lanes], sems.at[head])

    copies = [pltpu.make_async_copy(kv_hbm, kv_ref, kv_sems.at[YS])]
    for dy, source in enumerate((a0_ref, a1_ref, a2_ref, a3_ref)):
        first = (y + YS - dy) % YS * SIDES
        copies.append(pltpu.make_async_copy(source, anchor_ref.at[pl.ds(first, SIDES)], kv_sems.at[dy]))
    for copy in copies:
        copy.start()
    for head in range(KV_HEADS):
        copy_in(head).start()
    filler = jnp.where(place_ref[0] > 0, 0, BLOCK)
    row = lax.broadcasted_iota(jnp.int32, (BLOCK, 2 * BLOCK), 0)
    column = lax.broadcasted_iota(jnp.int32, (BLOCK, 2 * BLOCK), 1)
    allowed = (column >= filler) & (column <= row + BLOCK)
    for copy in copies:
        copy.wait()

    def one_head(head, carry):
        copy_in(head).wait()
        kv_lanes = pl.ds(pl.multiple_of(head * D, D), D)
        keys = jnp.concatenate([anchor_ref[head, A_K:A_K + BLOCK, :], kv_ref[0, :, kv_lanes]], 0)
        values = jnp.concatenate([anchor_ref[head, A_V:A_V + BLOCK, :], kv_ref[1, :, kv_lanes]], 0)
        for first in range(0, GROUP, STACK):
            lanes = [pl.ds(pl.multiple_of(head * width + (first + j) * D, D), D) for j in range(STACK)]
            queries = jnp.concatenate([q_ref[:, each] for each in lanes], 0)
            scores = dot_nt(queries, keys).reshape(STACK, BLOCK, 2 * BLOCK)
            scores = jnp.where(allowed[None], scores, FILLER)
            highest = jnp.max(scores, 2, keepdims=True)
            weights = jnp.exp2((scores - highest) * SCALE)
            total = jnp.sum(weights, 2, keepdims=True)
            summed = dot_nn(weights.astype(BF16).reshape(STACK * BLOCK, 2 * BLOCK), values)
            attended = (summed.reshape(STACK, BLOCK, D) / total).astype(BF16)
            for j in range(STACK):
                out_ref[:, lanes[j]] = attended[j]
        copy_out(head).start()
        return carry

    lax.fori_loop(0, KV_HEADS, one_head, 0)
    for head in range(KV_HEADS):
        copy_out(head).wait()


def merge_kernel(in_ref, out_ref):
    diagonal = (
        lax.broadcasted_iota(jnp.int32, (KV_HEADS, QROWS, D), 1)
        == lax.broadcasted_iota(jnp.int32, (KV_HEADS, QROWS, D), 2)
    )
    received = in_ref[...].reshape(YS, PAIRS, SIDES, B_ROWS, D)
    logs = []
    for pair in range(PAIRS):
        parts = received[:, pair, :, B_S:, :].reshape(KV_HEADS, B_ROWS - B_S, D)
        logs.append(parts[:, 0:1, :] + parts[:, 1:2, :] + parts[:, 2:3, :])
    highest = functools.reduce(jnp.maximum, logs)
    shares = [jnp.exp2(log - highest) for log in logs]
    whole = functools.reduce(jnp.add, shares)
    merged = jnp.zeros((KV_HEADS, QROWS, D), F32)
    for pair in range(PAIRS):
        share = jnp.sum(jnp.where(diagonal, shares[pair] / whole, 0.0), 2, keepdims=True)
        merged = merged + share * received[:, pair, :, 0:QROWS, :].reshape(KV_HEADS, QROWS, D)
    for head in range(KV_HEADS):
        for j in range(GROUP):
            first = (head * GROUP + j) * D
            out_ref[:, first:first + D] = merged[head, j * ROWS:(j + 1) * ROWS, :].astype(BF16)


VMEM = pl.BlockSpec(memory_space=pltpu.VMEM)
ANY = pl.BlockSpec(memory_space=pl.ANY)
SMEM = pl.BlockSpec(memory_space=pltpu.SMEM)
HBM = pl.BlockSpec(memory_space=pltpu.HBM)
PARAMS = pltpu.CompilerParams(vmem_limit_bytes=32 * 1024 * 1024)


def cost(flops, nbytes):
    return pl.CostEstimate(flops=flops, bytes_accessed=nbytes, transcendentals=0)


def at(y, z):
    return y * PAIRS * SIDES + z


ALL = [(y, z) for y in range(YS) for z in range(PAIRS * SIDES)]


def fan_along_z(piece):
    result = piece
    for step in (2, 6, 4):
        pairs = [(at(y, side), at(y, side + step)) for y in range(YS) for side in range(SIDES)]
        result = result + lax.ppermute(piece, "ctx", pairs)
    return result


def step_in_pair(array, dy, flip):
    return lax.ppermute(array, "ctx", [(at(y, z), at((y + dy) % YS, z ^ flip)) for y, z in ALL])


def per_device(context_q, context_key_value, query_token_queries, query_key_value):
    index = lax.axis_index("ctx")
    place = index.astype(jnp.int32).reshape(1)
    y, side = index // (PAIRS * SIDES), index % SIDES
    *packed_kv, packed_q = pl.pallas_call(
        pack_kernel,
        out_shape=(jax.ShapeDtypeStruct((A_ROWS, D), BF16),) * KV_HEADS
        + (jax.ShapeDtypeStruct((CTX, QROWS, D), BF16),),
        in_specs=[SMEM, HBM, HBM, HBM],
        out_specs=(VMEM,) * (KV_HEADS + 1),
        scratch_shapes=[
            pltpu.VMEM(context_key_value.shape, BF16),
            pltpu.VMEM(query_token_queries.shape, BF16),
            pltpu.VMEM(query_key_value.shape, BF16),
            pltpu.SemaphoreType.DMA((3,)),
        ],
        compiler_params=pltpu.CompilerParams(vmem_limit_bytes=56 * 1024 * 1024),
        cost_estimate=cost(0, 1 << 21),
    )(place, context_key_value, query_token_queries, query_key_value)
    queries = lax.all_to_all(packed_q, "ctx", 0, 0)
    kv = [packed_kv[0]] + [step_in_pair(packed_kv[n], *STEPS[n]) for n in range(1, KV_HEADS)]
    in_first = index // SIDES % PAIRS == 0
    piece = sum(
        jnp.where(in_first & (y == dy) & (side == flip), kv[n][:2 * BLOCK], 0)
        for n, (dy, flip) in enumerate(STEPS)
    )
    piece = fan_along_z(piece)
    other = step_in_pair(piece, 0, 1)
    partial = pl.pallas_call(
        query_kernel,
        out_shape=jax.ShapeDtypeStruct((CTX, B_ROWS, D), F32),
        in_specs=[SMEM] + [VMEM] * (KV_HEADS + 1),
        out_specs=VMEM,
        compiler_params=PARAMS,
        cost_estimate=cost(1 << 29, 1 << 21),
    )(place, *kv, queries)
    halved = partial.astype(jnp.float16)
    halved, piece = lax.optimization_barrier((halved, piece))
    both = jnp.stack([jnp.where(side == 0, piece, other), jnp.where(side == 0, other, piece)])
    pieces = [both] + [step_in_pair(both, dy, 0) for dy in range(1, YS)]
    gathered = lax.all_to_all(halved, "ctx", 0, 0).astype(F32)
    context_out = pl.pallas_call(
        encode_kernel,
        out_shape=jax.ShapeDtypeStruct(context_q.shape, BF16),
        in_specs=[SMEM, HBM, HBM] + [VMEM] * YS,
        out_specs=HBM,
        scratch_shapes=[
            pltpu.VMEM(context_q.shape, BF16),
            pltpu.VMEM(context_key_value.shape, BF16),
            pltpu.VMEM((KV_HEADS, 2 * BLOCK, D), BF16),
            pltpu.VMEM(context_q.shape, BF16),
            pltpu.SemaphoreType.DMA((KV_HEADS,)),
            pltpu.SemaphoreType.DMA((YS + 1,)),
            pltpu.SemaphoreType.DMA((KV_HEADS,)),
        ],
        compiler_params=pltpu.CompilerParams(vmem_limit_bytes=52 * 1024 * 1024),
        cost_estimate=cost(1 << 36, 1 << 24),
    )(place, context_q, context_key_value, *pieces)
    query_out = pl.pallas_call(
        merge_kernel,
        out_shape=jax.ShapeDtypeStruct(query_token_queries.shape, BF16),
        in_specs=[VMEM],
        out_specs=VMEM,
        compiler_params=PARAMS,
        cost_estimate=cost(1 << 20, 1 << 20),
    )(gathered)
    return context_out, query_out


def solution(mesh):
    return jax.shard_map(
        per_device,
        mesh=mesh,
        in_specs=(
            P(("req", "ctx"), None),
            P(None, ("req", "ctx"), None),
            P(("req", "ctx"), None),
            P(None, ("req", "ctx"), None),
        ),
        out_specs=(P(("req", "ctx"), None), P(("req", "ctx"), None)),
        check_vma=False,
    )
```

```python
import functools

import jax
import jax.numpy as jnp
from jax import lax
from jax.experimental import pallas as pl
from jax.experimental.pallas import tpu as pltpu
from jax.sharding import PartitionSpec as P

KV_HEADS = 8
GROUP = 8
D = 128
BLOCK = 128
YS = 4
PAIRS = 4
SIDES = 2
CTX = YS * PAIRS * SIDES
ROWS = 4
QROWS = ROWS * GROUP
F32 = jnp.float32
BF16 = jnp.bfloat16
FILLER = -1e30
LOG2E = 1.4426950408889634
SCALE = D ** -0.5 * LOG2E

FAR = 2
STEPS = [(dy, flip) for dy in range(YS) for flip in range(SIDES)]
A_K, A_V, A_SK, A_SV = 0, BLOCK, 2 * BLOCK, 2 * BLOCK + 8
A_ROWS = A_SV + 8
B_S = QROWS
B_ROWS = B_S + 8


def dot_nt(a, b):
    return lax.dot_general(a, b, (((1,), (1,)), ((), ())), preferred_element_type=F32)


def dot_nn(a, b):
    return lax.dot_general(a, b, (((1,), (0,)), ((), ())), preferred_element_type=F32)


def side_of(place):
    return (place + jnp.where(place // SIDES % PAIRS == FAR, 1, 0)) % SIDES


def place_of(y, pair, side):
    swapped = (side + (pair == FAR)) % SIDES
    return y * (PAIRS * SIDES) + pair * SIDES + swapped


def pack_kernel(place_ref, kv_hbm, q_hbm, qkv_hbm, *refs):
    kv_out_refs, (q_out_ref, kv_ref, q_ref, qkv_ref, sems) = refs[:KV_HEADS], refs[KV_HEADS:]
    copies = [
        pltpu.make_async_copy(source, target, sems.at[i])
        for i, (source, target) in enumerate(((q_hbm, q_ref), (qkv_hbm, qkv_ref), (kv_hbm, kv_ref)))
    ]
    for copy in copies:
        copy.start()
    for copy in copies:
        copy.wait()
    q = q_ref[...].astype(F32)
    for head in range(KV_HEADS):
        first = head * GROUP * D
        queries = jnp.concatenate(
            [q[:, first + j * D:first + (j + 1) * D] for j in range(GROUP)], 0
        ).astype(BF16)
        for pair in range(PAIRS):
            q_out_ref[place_of(head // SIDES, pair, head % SIDES)] = queries
    y, side = place_ref[0] // (PAIRS * SIDES), side_of(place_ref[0])
    blank = jnp.zeros((8 - ROWS, D), F32)
    for (dy, flip), out_ref in zip(STEPS, kv_out_refs):
        head = (y + dy) % YS * SIDES + (side + flip) % SIDES
        lanes = pl.ds(pl.multiple_of(head * D, D), D)
        out_ref[A_K:A_K + BLOCK, :] = kv_ref[0, :, lanes]
        out_ref[A_V:A_V + BLOCK, :] = kv_ref[1, :, lanes]
        out_ref[A_SK:A_ROWS, :] = jnp.concatenate(
            [qkv_ref[0, :, lanes].astype(F32), blank, qkv_ref[1, :, lanes].astype(F32), blank], 0
        ).astype(BF16)


CHUNK = 8
STACK = 4


def query_kernel(place_ref, *refs):
    kv_refs, (q_ref, out_ref) = refs[:KV_HEADS], refs[KV_HEADS:]
    place = place_ref[0]
    y, pair, side = place // (PAIRS * SIDES), place // SIDES % PAIRS, side_of(place)
    keys = jnp.concatenate([ref[A_K:A_K + BLOCK, :] for ref in kv_refs], 0)
    values = jnp.concatenate([ref[A_V:A_V + BLOCK, :] for ref in kv_refs], 0)
    tails = [ref[A_SK:A_ROWS, :].astype(F32) for ref in kv_refs]
    self_keys = jnp.concatenate([tail[0:8] for tail in tails], 0).astype(BF16)
    self_values = jnp.concatenate([tail[8:16] for tail in tails], 0).astype(BF16)
    rows = CHUNK * QROWS
    row_id = lax.broadcasted_iota(jnp.int32, (rows, KV_HEADS * 8), 0)
    column = lax.broadcasted_iota(jnp.int32, (rows, KV_HEADS * 8), 1)
    source, key_row = column // 8, column % 8
    source_y, source_side = (y + YS - source // SIDES) % YS, (side + source % SIDES) % SIDES
    source_side = (source_side + jnp.where(pair == FAR, 1, 0)) % SIDES
    key_pos = (source_y * (PAIRS * SIDES) + pair * SIDES + source_side) * ROWS + key_row
    key_pos = jnp.where(key_row < ROWS, key_pos, CTX * ROWS)
    row_pos = (row_id // QROWS) * ROWS + row_id % ROWS
    diagonal = (
        lax.broadcasted_iota(jnp.int32, (CHUNK, QROWS, D), 1)
        == lax.broadcasted_iota(jnp.int32, (CHUNK, QROWS, D), 2)
    )
    for chunk in range(CTX // CHUNK):
        sources = slice(chunk * CHUNK, (chunk + 1) * CHUNK)
        queries = q_ref[sources].reshape(rows, D)
        scores = dot_nt(queries, keys)
        self_scores = dot_nt(queries, self_keys)
        self_scores = jnp.where(key_pos <= row_pos + chunk * CHUNK * ROWS, self_scores, FILLER)
        highest = jnp.maximum(jnp.max(scores, 1, keepdims=True), jnp.max(self_scores, 1, keepdims=True))
        weights = jnp.exp2((scores - highest) * SCALE)
        self_weights = jnp.exp2((self_scores - highest) * SCALE)
        total = jnp.sum(weights, 1, keepdims=True) + jnp.sum(self_weights, 1, keepdims=True)
        summed = dot_nn(weights.astype(BF16), values) + dot_nn(self_weights.astype(BF16), self_values)
        out_ref[sources, 0:QROWS, :] = (summed / total).reshape(CHUNK, QROWS, D)
        log_sum = (highest * SCALE + jnp.log2(total)).reshape(CHUNK, QROWS, 1)
        log_row = jnp.sum(jnp.where(diagonal, log_sum, 0.0), 1, keepdims=True)
        first = log_row.astype(BF16).astype(F32)
        second = (log_row - first).astype(BF16).astype(F32)
        third = log_row - first - second
        out_ref[sources, B_S:B_ROWS, :] = jnp.concatenate(
            [first, second, third, jnp.zeros((CHUNK, 5, D), F32)], 1
        )


def encode_kernel(
    place_ref, q_hbm, kv_hbm, a0_ref, a1_ref, a2_ref, a3_ref, out_hbm,
    q_ref, kv_ref, anchor_ref, out_ref, q_sems, kv_sems, sems
):
    width = GROUP * D
    y = place_ref[0] // (PAIRS * SIDES)

    def copy_in(head):
        lanes = pl.ds(pl.multiple_of(head * width, width), width)
        return pltpu.make_async_copy(q_hbm.at[:, lanes], q_ref.at[:, lanes], q_sems.at[head])

    def copy_out(head):
        lanes = pl.ds(pl.multiple_of(head * width, width), width)
        return pltpu.make_async_copy(out_ref.at[:, lanes], out_hbm.at[:, lanes], sems.at[head])

    copies = [pltpu.make_async_copy(kv_hbm, kv_ref, kv_sems.at[YS])]
    for dy, source in enumerate((a0_ref, a1_ref, a2_ref, a3_ref)):
        first = (y + YS - dy) % YS * SIDES
        copies.append(pltpu.make_async_copy(source, anchor_ref.at[pl.ds(first, SIDES)], kv_sems.at[dy]))
    for copy in copies:
        copy.start()
    for head in range(KV_HEADS):
        copy_in(head).start()
    filler = jnp.where(place_ref[0] > 0, 0, BLOCK)
    row = lax.broadcasted_iota(jnp.int32, (BLOCK, 2 * BLOCK), 0)
    column = lax.broadcasted_iota(jnp.int32, (BLOCK, 2 * BLOCK), 1)
    allowed = (column >= filler) & (column <= row + BLOCK)
    for copy in copies:
        copy.wait()

    def one_head(head, carry):
        copy_in(head).wait()
        kv_lanes = pl.ds(pl.multiple_of(head * D, D), D)
        keys = jnp.concatenate([anchor_ref[head, A_K:A_K + BLOCK, :], kv_ref[0, :, kv_lanes]], 0)
        values = jnp.concatenate([anchor_ref[head, A_V:A_V + BLOCK, :], kv_ref[1, :, kv_lanes]], 0)
        for first in range(0, GROUP, STACK):
            lanes = [pl.ds(pl.multiple_of(head * width + (first + j) * D, D), D) for j in range(STACK)]
            queries = jnp.concatenate([q_ref[:, each] for each in lanes], 0)
            scores = dot_nt(queries, keys).reshape(STACK, BLOCK, 2 * BLOCK)
            scores = jnp.where(allowed[None], scores, FILLER)
            highest = jnp.max(scores, 2, keepdims=True)
            weights = jnp.exp2((scores - highest) * SCALE)
            total = jnp.sum(weights, 2, keepdims=True)
            summed = dot_nn(weights.astype(BF16).reshape(STACK * BLOCK, 2 * BLOCK), values)
            attended = (summed.reshape(STACK, BLOCK, D) / total).astype(BF16)
            for j in range(STACK):
                out_ref[:, lanes[j]] = attended[j]
        copy_out(head).start()
        return carry

    lax.fori_loop(0, KV_HEADS, one_head, 0)
    for head in range(KV_HEADS):
        copy_out(head).wait()


def merge_kernel(in_ref, out_ref):
    diagonal = (
        lax.broadcasted_iota(jnp.int32, (KV_HEADS, QROWS, D), 1)
        == lax.broadcasted_iota(jnp.int32, (KV_HEADS, QROWS, D), 2)
    )
    received = in_ref[...].reshape(YS, PAIRS, SIDES, B_ROWS, D)
    received = [received[:, pair] for pair in range(PAIRS)]
    received[FAR] = jnp.concatenate([received[FAR][:, 1:2], received[FAR][:, 0:1]], 1)
    logs = []
    for pair in range(PAIRS):
        parts = received[pair][:, :, B_S:, :].reshape(KV_HEADS, B_ROWS - B_S, D)
        logs.append(parts[:, 0:1, :] + parts[:, 1:2, :] + parts[:, 2:3, :])
    highest = functools.reduce(jnp.maximum, logs)
    shares = [jnp.exp2(log - highest) for log in logs]
    whole = functools.reduce(jnp.add, shares)
    merged = jnp.zeros((KV_HEADS, QROWS, D), F32)
    for pair in range(PAIRS):
        share = jnp.sum(jnp.where(diagonal, shares[pair] / whole, 0.0), 2, keepdims=True)
        merged = merged + share * received[pair][:, :, 0:QROWS, :].reshape(KV_HEADS, QROWS, D)
    for head in range(KV_HEADS):
        for j in range(GROUP):
            first = (head * GROUP + j) * D
            out_ref[:, first:first + D] = merged[head, j * ROWS:(j + 1) * ROWS, :].astype(BF16)


VMEM = pl.BlockSpec(memory_space=pltpu.VMEM)
ANY = pl.BlockSpec(memory_space=pl.ANY)
SMEM = pl.BlockSpec(memory_space=pltpu.SMEM)
HBM = pl.BlockSpec(memory_space=pltpu.HBM)
PARAMS = pltpu.CompilerParams(vmem_limit_bytes=32 * 1024 * 1024)


def cost(flops, nbytes):
    return pl.CostEstimate(flops=flops, bytes_accessed=nbytes, transcendentals=0)


def at(y, z):
    return y * PAIRS * SIDES + z


ALL = [(y, z) for y in range(YS) for z in range(PAIRS * SIDES)]


def fan_along_z(piece):
    result = piece
    for pair in (1, 3, FAR):
        pairs = [(place_of(y, 0, side), place_of(y, pair, side)) for y in range(YS) for side in range(SIDES)]
        result = result + lax.ppermute(piece, "ctx", pairs)
    return result


def step_in_pair(array, dy, flip):
    return lax.ppermute(array, "ctx", [(at(y, z), at((y + dy) % YS, z ^ flip)) for y, z in ALL])


def per_device(context_q, context_key_value, query_token_queries, query_key_value):
    index = lax.axis_index("ctx")
    place = index.astype(jnp.int32).reshape(1)
    y, side = index // (PAIRS * SIDES), side_of(index)
    *packed_kv, packed_q = pl.pallas_call(
        pack_kernel,
        out_shape=(jax.ShapeDtypeStruct((A_ROWS, D), BF16),) * KV_HEADS
        + (jax.ShapeDtypeStruct((CTX, QROWS, D), BF16),),
        in_specs=[SMEM, HBM, HBM, HBM],
        out_specs=(VMEM,) * (KV_HEADS + 1),
        scratch_shapes=[
            pltpu.VMEM(context_key_value.shape, BF16),
            pltpu.VMEM(query_token_queries.shape, BF16),
            pltpu.VMEM(query_key_value.shape, BF16),
            pltpu.SemaphoreType.DMA((3,)),
        ],
        compiler_params=pltpu.CompilerParams(vmem_limit_bytes=56 * 1024 * 1024),
        cost_estimate=cost(0, 1 << 21),
    )(place, context_key_value, query_token_queries, query_key_value)
    queries = lax.all_to_all(packed_q, "ctx", 0, 0)
    kv = [packed_kv[0]] + [step_in_pair(packed_kv[n], *STEPS[n]) for n in range(1, KV_HEADS)]
    in_first = index // SIDES % PAIRS == 0
    piece = sum(
        jnp.where(in_first & (y == dy) & (side == flip), kv[n][:2 * BLOCK], 0)
        for n, (dy, flip) in enumerate(STEPS)
    )
    piece = fan_along_z(piece)
    other = step_in_pair(piece, 0, 1)
    partial = pl.pallas_call(
        query_kernel,
        out_shape=jax.ShapeDtypeStruct((CTX, B_ROWS, D), F32),
        in_specs=[SMEM] + [VMEM] * (KV_HEADS + 1),
        out_specs=VMEM,
        compiler_params=PARAMS,
        cost_estimate=cost(1 << 29, 1 << 21),
    )(place, *kv, queries)
    halved = partial.astype(jnp.float16)
    halved, piece = lax.optimization_barrier((halved, piece))
    both = jnp.stack([jnp.where(side == 0, piece, other), jnp.where(side == 0, other, piece)])
    pieces = [both] + [step_in_pair(both, dy, 0) for dy in range(1, YS)]
    gathered = lax.all_to_all(halved, "ctx", 0, 0).astype(F32)
    context_out = pl.pallas_call(
        encode_kernel,
        out_shape=jax.ShapeDtypeStruct(context_q.shape, BF16),
        in_specs=[SMEM, HBM, HBM] + [VMEM] * YS,
        out_specs=HBM,
        scratch_shapes=[
            pltpu.VMEM(context_q.shape, BF16),
            pltpu.VMEM(context_key_value.shape, BF16),
            pltpu.VMEM((KV_HEADS, 2 * BLOCK, D), BF16),
            pltpu.VMEM(context_q.shape, BF16),
            pltpu.SemaphoreType.DMA((KV_HEADS,)),
            pltpu.SemaphoreType.DMA((YS + 1,)),
            pltpu.SemaphoreType.DMA((KV_HEADS,)),
        ],
        compiler_params=pltpu.CompilerParams(vmem_limit_bytes=52 * 1024 * 1024),
        cost_estimate=cost(1 << 36, 1 << 24),
    )(place, context_q, context_key_value, *pieces)
    query_out = pl.pallas_call(
        merge_kernel,
        out_shape=jax.ShapeDtypeStruct(query_token_queries.shape, BF16),
        in_specs=[VMEM],
        out_specs=VMEM,
        compiler_params=PARAMS,
        cost_estimate=cost(1 << 20, 1 << 20),
    )(gathered)
    return context_out, query_out


def solution(mesh):
    return jax.shard_map(
        per_device,
        mesh=mesh,
        in_specs=(
            P(("req", "ctx"), None),
            P(None, ("req", "ctx"), None),
            P(("req", "ctx"), None),
            P(None, ("req", "ctx"), None),
        ),
        out_specs=(P(("req", "ctx"), None), P(("req", "ctx"), None)),
        check_vma=False,
    )
```

```python
import functools

import jax
import jax.numpy as jnp
from jax import lax
from jax.experimental import pallas as pl
from jax.experimental.pallas import tpu as pltpu
from jax.sharding import PartitionSpec as P

KV_HEADS = 8
GROUP = 8
D = 128
BLOCK = 128
YS = 4
PAIRS = 4
SIDES = 2
CTX = YS * PAIRS * SIDES
ROWS = 4
QROWS = ROWS * GROUP
F32 = jnp.float32
BF16 = jnp.bfloat16
FILLER = -1e30
LOG2E = 1.4426950408889634
SCALE = D ** -0.5 * LOG2E

FAR = 2
STEPS = [(dy, flip) for dy in range(YS) for flip in range(SIDES)]
A_K, A_V, A_SK, A_SV = 0, BLOCK, 2 * BLOCK, 2 * BLOCK + 8
A_ROWS = A_SV + 8
B_S = QROWS
B_ROWS = B_S + 8


def dot_nt(a, b):
    return lax.dot_general(a, b, (((1,), (1,)), ((), ())), preferred_element_type=F32)


def dot_nn(a, b):
    return lax.dot_general(a, b, (((1,), (0,)), ((), ())), preferred_element_type=F32)


def side_of(place):
    return (place + jnp.where(place // SIDES % PAIRS == FAR, 1, 0)) % SIDES


def place_of(y, pair, side):
    swapped = (side + (pair == FAR)) % SIDES
    return y * (PAIRS * SIDES) + pair * SIDES + swapped


def pack_kernel(place_ref, kv_hbm, q_hbm, qkv_hbm, *refs):
    kv_out_refs, (q_out_ref, kv_ref, q_ref, qkv_ref, sems) = refs[:KV_HEADS], refs[KV_HEADS:]
    copies = [
        pltpu.make_async_copy(source, target, sems.at[i])
        for i, (source, target) in enumerate(((q_hbm, q_ref), (qkv_hbm, qkv_ref), (kv_hbm, kv_ref)))
    ]
    for copy in copies:
        copy.start()
    for copy in copies:
        copy.wait()
    q = q_ref[...].astype(F32)
    for head in range(KV_HEADS):
        first = head * GROUP * D
        queries = jnp.concatenate(
            [q[:, first + j * D:first + (j + 1) * D] for j in range(GROUP)], 0
        ).astype(BF16)
        for pair in range(PAIRS):
            q_out_ref[place_of(head // SIDES, pair, head % SIDES)] = queries
    y, side = place_ref[0] // (PAIRS * SIDES), side_of(place_ref[0])
    blank = jnp.zeros((8 - ROWS, D), F32)
    for (dy, flip), out_ref in zip(STEPS, kv_out_refs):
        head = (y + dy) % YS * SIDES + (side + flip) % SIDES
        lanes = pl.ds(pl.multiple_of(head * D, D), D)
        out_ref[A_K:A_K + BLOCK, :] = kv_ref[0, :, lanes]
        out_ref[A_V:A_V + BLOCK, :] = kv_ref[1, :, lanes]
        out_ref[A_SK:A_ROWS, :] = jnp.concatenate(
            [qkv_ref[0, :, lanes].astype(F32), blank, qkv_ref[1, :, lanes].astype(F32), blank], 0
        ).astype(BF16)


CHUNK = 16
STACK = 4


def query_kernel(place_ref, *refs):
    kv_refs, (q_ref, out_ref) = refs[:KV_HEADS], refs[KV_HEADS:]
    place = place_ref[0]
    y, pair, side = place // (PAIRS * SIDES), place // SIDES % PAIRS, side_of(place)
    keys = jnp.concatenate([ref[A_K:A_K + BLOCK, :] for ref in kv_refs], 0)
    values = jnp.concatenate([ref[A_V:A_V + BLOCK, :] for ref in kv_refs], 0)
    tails = [ref[A_SK:A_ROWS, :].astype(F32) for ref in kv_refs]
    self_keys = jnp.concatenate([tail[0:8] for tail in tails], 0).astype(BF16)
    self_values = jnp.concatenate([tail[8:16] for tail in tails], 0).astype(BF16)
    rows = CHUNK * QROWS
    row_id = lax.broadcasted_iota(jnp.int32, (rows, KV_HEADS * 8), 0)
    column = lax.broadcasted_iota(jnp.int32, (rows, KV_HEADS * 8), 1)
    source, key_row = column // 8, column % 8
    source_y, source_side = (y + YS - source // SIDES) % YS, (side + source % SIDES) % SIDES
    source_side = (source_side + jnp.where(pair == FAR, 1, 0)) % SIDES
    key_pos = (source_y * (PAIRS * SIDES) + pair * SIDES + source_side) * ROWS + key_row
    key_pos = jnp.where(key_row < ROWS, key_pos, CTX * ROWS)
    row_pos = (row_id // QROWS) * ROWS + row_id % ROWS
    diagonal = (
        lax.broadcasted_iota(jnp.int32, (CHUNK, QROWS, D), 1)
        == lax.broadcasted_iota(jnp.int32, (CHUNK, QROWS, D), 2)
    )
    for chunk in range(CTX // CHUNK):
        sources = slice(chunk * CHUNK, (chunk + 1) * CHUNK)
        queries = q_ref[sources].reshape(rows, D)
        scores = dot_nt(queries, keys)
        self_scores = dot_nt(queries, self_keys)
        self_scores = jnp.where(key_pos <= row_pos + chunk * CHUNK * ROWS, self_scores, FILLER)
        highest = jnp.maximum(jnp.max(scores, 1, keepdims=True), jnp.max(self_scores, 1, keepdims=True))
        weights = jnp.exp2((scores - highest) * SCALE)
        self_weights = jnp.exp2((self_scores - highest) * SCALE)
        total = jnp.sum(weights, 1, keepdims=True) + jnp.sum(self_weights, 1, keepdims=True)
        summed = dot_nn(weights.astype(BF16), values) + dot_nn(self_weights.astype(BF16), self_values)
        out_ref[sources, 0:QROWS, :] = (summed / total).reshape(CHUNK, QROWS, D)
        log_sum = (highest * SCALE + jnp.log2(total)).reshape(CHUNK, QROWS, 1)
        log_row = jnp.sum(jnp.where(diagonal, log_sum, 0.0), 1, keepdims=True)
        first = log_row.astype(BF16).astype(F32)
        second = (log_row - first).astype(BF16).astype(F32)
        third = log_row - first - second
        out_ref[sources, B_S:B_ROWS, :] = jnp.concatenate(
            [first, second, third, jnp.zeros((CHUNK, 5, D), F32)], 1
        )


def encode_kernel(
    place_ref, q_hbm, kv_hbm, a0_ref, a1_ref, a2_ref, a3_ref, out_hbm,
    q_ref, kv_ref, anchor_ref, out_ref, q_sems, kv_sems, sems
):
    width = GROUP * D
    y = place_ref[0] // (PAIRS * SIDES)

    def copy_in(head):
        lanes = pl.ds(pl.multiple_of(head * width, width), width)
        return pltpu.make_async_copy(q_hbm.at[:, lanes], q_ref.at[:, lanes], q_sems.at[head])

    def copy_out(head):
        lanes = pl.ds(pl.multiple_of(head * width, width), width)
        return pltpu.make_async_copy(out_ref.at[:, lanes], out_hbm.at[:, lanes], sems.at[head])

    copies = [pltpu.make_async_copy(kv_hbm, kv_ref, kv_sems.at[YS])]
    for dy, source in enumerate((a0_ref, a1_ref, a2_ref, a3_ref)):
        first = (y + YS - dy) % YS * SIDES
        copies.append(pltpu.make_async_copy(source, anchor_ref.at[pl.ds(first, SIDES)], kv_sems.at[dy]))
    for copy in copies:
        copy.start()
    for head in range(KV_HEADS):
        copy_in(head).start()
    filler = jnp.where(place_ref[0] > 0, 0, BLOCK)
    row = lax.broadcasted_iota(jnp.int32, (BLOCK, 2 * BLOCK), 0)
    column = lax.broadcasted_iota(jnp.int32, (BLOCK, 2 * BLOCK), 1)
    allowed = (column >= filler) & (column <= row + BLOCK)
    for copy in copies:
        copy.wait()

    def one_head(head, carry):
        copy_in(head).wait()
        kv_lanes = pl.ds(pl.multiple_of(head * D, D), D)
        keys = jnp.concatenate([anchor_ref[head, A_K:A_K + BLOCK, :], kv_ref[0, :, kv_lanes]], 0)
        values = jnp.concatenate([anchor_ref[head, A_V:A_V + BLOCK, :], kv_ref[1, :, kv_lanes]], 0)
        for first in range(0, GROUP, STACK):
            lanes = [pl.ds(pl.multiple_of(head * width + (first + j) * D, D), D) for j in range(STACK)]
            queries = jnp.concatenate([q_ref[:, each] for each in lanes], 0)
            scores = dot_nt(queries, keys).reshape(STACK, BLOCK, 2 * BLOCK)
            scores = jnp.where(allowed[None], scores, FILLER)
            highest = jnp.max(scores, 2, keepdims=True)
            weights = jnp.exp2((scores - highest) * SCALE)
            total = jnp.sum(weights, 2, keepdims=True)
            summed = dot_nn(weights.astype(BF16).reshape(STACK * BLOCK, 2 * BLOCK), values)
            attended = (summed.reshape(STACK, BLOCK, D) / total).astype(BF16)
            for j in range(STACK):
                out_ref[:, lanes[j]] = attended[j]
        copy_out(head).start()
        return carry

    lax.fori_loop(0, KV_HEADS, one_head, 0)
    for head in range(KV_HEADS):
        copy_out(head).wait()


def merge_kernel(in_ref, out_ref):
    diagonal = (
        lax.broadcasted_iota(jnp.int32, (KV_HEADS, QROWS, D), 1)
        == lax.broadcasted_iota(jnp.int32, (KV_HEADS, QROWS, D), 2)
    )
    received = in_ref[...].reshape(YS, PAIRS, SIDES, B_ROWS, D)
    received = [received[:, pair] for pair in range(PAIRS)]
    received[FAR] = jnp.concatenate([received[FAR][:, 1:2], received[FAR][:, 0:1]], 1)
    logs = []
    for pair in range(PAIRS):
        parts = received[pair][:, :, B_S:, :].reshape(KV_HEADS, B_ROWS - B_S, D)
        logs.append(parts[:, 0:1, :] + parts[:, 1:2, :] + parts[:, 2:3, :])
    highest = functools.reduce(jnp.maximum, logs)
    shares = [jnp.exp2(log - highest) for log in logs]
    whole = functools.reduce(jnp.add, shares)
    merged = jnp.zeros((KV_HEADS, QROWS, D), F32)
    for pair in range(PAIRS):
        share = jnp.sum(jnp.where(diagonal, shares[pair] / whole, 0.0), 2, keepdims=True)
        merged = merged + share * received[pair][:, :, 0:QROWS, :].reshape(KV_HEADS, QROWS, D)
    for head in range(KV_HEADS):
        for j in range(GROUP):
            first = (head * GROUP + j) * D
            out_ref[:, first:first + D] = merged[head, j * ROWS:(j + 1) * ROWS, :].astype(BF16)


VMEM = pl.BlockSpec(memory_space=pltpu.VMEM)
ANY = pl.BlockSpec(memory_space=pl.ANY)
SMEM = pl.BlockSpec(memory_space=pltpu.SMEM)
HBM = pl.BlockSpec(memory_space=pltpu.HBM)
PARAMS = pltpu.CompilerParams(vmem_limit_bytes=32 * 1024 * 1024)


def cost(flops, nbytes):
    return pl.CostEstimate(flops=flops, bytes_accessed=nbytes, transcendentals=0)


def at(y, z):
    return y * PAIRS * SIDES + z


ALL = [(y, z) for y in range(YS) for z in range(PAIRS * SIDES)]


def fan_along_z(piece):
    result = piece
    for pair in (1, 3, FAR):
        pairs = [(place_of(y, 0, side), place_of(y, pair, side)) for y in range(YS) for side in range(SIDES)]
        result = result + lax.ppermute(piece, "ctx", pairs)
    return result


def step_in_pair(array, dy, flip):
    return lax.ppermute(array, "ctx", [(at(y, z), at((y + dy) % YS, z ^ flip)) for y, z in ALL])


def per_device(context_q, context_key_value, query_token_queries, query_key_value):
    index = lax.axis_index("ctx")
    place = index.astype(jnp.int32).reshape(1)
    y, side = index // (PAIRS * SIDES), side_of(index)
    *packed_kv, packed_q = pl.pallas_call(
        pack_kernel,
        out_shape=(jax.ShapeDtypeStruct((A_ROWS, D), BF16),) * KV_HEADS
        + (jax.ShapeDtypeStruct((CTX, QROWS, D), BF16),),
        in_specs=[SMEM, HBM, HBM, HBM],
        out_specs=(VMEM,) * (KV_HEADS + 1),
        scratch_shapes=[
            pltpu.VMEM(context_key_value.shape, BF16),
            pltpu.VMEM(query_token_queries.shape, BF16),
            pltpu.VMEM(query_key_value.shape, BF16),
            pltpu.SemaphoreType.DMA((3,)),
        ],
        compiler_params=pltpu.CompilerParams(vmem_limit_bytes=56 * 1024 * 1024),
        cost_estimate=cost(0, 1 << 21),
    )(place, context_key_value, query_token_queries, query_key_value)
    queries = lax.all_to_all(packed_q, "ctx", 0, 0)
    kv = [packed_kv[0]] + [step_in_pair(packed_kv[n], *STEPS[n]) for n in range(1, KV_HEADS)]
    in_first = index // SIDES % PAIRS == 0
    piece = sum(
        jnp.where(in_first & (y == dy) & (side == flip), kv[n][:2 * BLOCK], 0)
        for n, (dy, flip) in enumerate(STEPS)
    )
    piece = fan_along_z(piece)
    other = step_in_pair(piece, 0, 1)
    partial = pl.pallas_call(
        query_kernel,
        out_shape=jax.ShapeDtypeStruct((CTX, B_ROWS, D), F32),
        in_specs=[SMEM] + [VMEM] * (KV_HEADS + 1),
        out_specs=VMEM,
        compiler_params=PARAMS,
        cost_estimate=cost(1 << 29, 1 << 21),
    )(place, *kv, queries)
    halved = partial.astype(jnp.float16)
    halved, piece = lax.optimization_barrier((halved, piece))
    both = jnp.stack([jnp.where(side == 0, piece, other), jnp.where(side == 0, other, piece)])
    pieces = [both] + [step_in_pair(both, dy, 0) for dy in range(1, YS)]
    gathered = lax.all_to_all(halved, "ctx", 0, 0).astype(F32)
    context_out = pl.pallas_call(
        encode_kernel,
        out_shape=jax.ShapeDtypeStruct(context_q.shape, BF16),
        in_specs=[SMEM, HBM, HBM] + [VMEM] * YS,
        out_specs=HBM,
        scratch_shapes=[
            pltpu.VMEM(context_q.shape, BF16),
            pltpu.VMEM(context_key_value.shape, BF16),
            pltpu.VMEM((KV_HEADS, 2 * BLOCK, D), BF16),
            pltpu.VMEM(context_q.shape, BF16),
            pltpu.SemaphoreType.DMA((KV_HEADS,)),
            pltpu.SemaphoreType.DMA((YS + 1,)),
            pltpu.SemaphoreType.DMA((KV_HEADS,)),
        ],
        compiler_params=pltpu.CompilerParams(vmem_limit_bytes=52 * 1024 * 1024),
        cost_estimate=cost(1 << 36, 1 << 24),
    )(place, context_q, context_key_value, *pieces)
    query_out = pl.pallas_call(
        merge_kernel,
        out_shape=jax.ShapeDtypeStruct(query_token_queries.shape, BF16),
        in_specs=[VMEM],
        out_specs=VMEM,
        compiler_params=PARAMS,
        cost_estimate=cost(1 << 20, 1 << 20),
    )(gathered)
    return context_out, query_out


def solution(mesh):
    return jax.shard_map(
        per_device,
        mesh=mesh,
        in_specs=(
            P(("req", "ctx"), None),
            P(None, ("req", "ctx"), None),
            P(("req", "ctx"), None),
            P(None, ("req", "ctx"), None),
        ),
        out_specs=(P(("req", "ctx"), None), P(("req", "ctx"), None)),
        check_vma=False,
    )
```
